32 devices in a mesh: seq: 8 (over z, core), tp: 4 (over y, x).
Axes of the slice: x: 2, y: 2, z: 4, core: 2. Of those that a mesh axis runs over, the one named last changes fastest.
Arguments:
- tokens: bfloat16 [4, 2048, 2048], P(None, 'seq'), may hold values from -6 to 6
- positions: int32 [4, 2048], P(None, 'seq'), may hold values from 0 to 2047, as said below
- w_query: bfloat16 [2048, 2048], P(None, 'tp'), may hold values from -0.1875 to 0.1875
- w_key: bfloat16 [2048, 2048], P(None, 'tp'), may hold values from -0.1875 to 0.1875
- w_value: bfloat16 [2048, 2048], P(None, 'tp'), may hold values from -0.125 to 0.125
- w_out: bfloat16 [2048, 2048], P('tp'), may hold values from -0.5 to 0.5
- w_gate: bfloat16 [2048, 5504], P(None, 'tp'), may hold values from -0.125 to 0.125
- w_up: bfloat16 [2048, 5504], P(None, 'tp'), may hold values from -0.125 to 0.125
- w_down: bfloat16 [5504, 2048], P('tp'), may hold values from -0.15625 to 0.15625
- gain_attn: float32 [2048], replicated, may hold values from 0.5 to 1.5
- gain_ffn: float32 [2048], replicated, may hold values from 0.5 to 1.5
- cotangent: bfloat16 [4, 2048, 2048], P(None, 'seq'), may hold values from -6 to 6
Outputs:
- output: bfloat16 [4, 2048, 2048], P(None, 'seq')
- token_grad: bfloat16 [4, 2048, 2048], P(None, 'seq')
- grad_query: float32 [2048, 2048], P(None, 'tp')
- grad_key: float32 [2048, 2048], P(None, 'tp')
- grad_value: float32 [2048, 2048], P(None, 'tp')
- grad_out: float32 [2048, 2048], P('tp')
- grad_gate: float32 [2048, 5504], P(None, 'tp')
- grad_up: float32 [2048, 5504], P(None, 'tp')
- grad_down: float32 [5504, 2048], P('tp')
- grad_gain_attn: float32 [2048], replicated
- grad_gain_ffn: float32 [2048], replicated
The draws below stay inside these ranges and needn't reach their ends.
Inputs may be any that keep to these rules, and one draw needn't show every extreme that they name: Each row of 2048 tokens is a pack of documents: positions are 0 at a document's first token and rise by one to its end; every row begins a document at its first token, and in every draw one row holds a document that begins among its first 256 tokens and runs to the row's end.
All inputs are finite; a program needn't handle non-finite values.
Results may differ from the reference program's by a relative error of at most 0.02.
Values may be sent and summed in bfloat16 or wider, within the bound.
No kernel may reach another device: no remote copies, remote signals or barrier semaphores. Data moves between devices by JAX's collectives and lax.ppermute only.
A program may use at most 320 MiB of HBM per device.

```python
import jax
import jax.numpy as jnp
from jax import lax

D = 2048
HEADS = 16
HEAD = 128
FF = 5504
WINDOW = 1024
ROW_LEN = 2048
GROUP = 256
ROWS = 4


def draw_positions(key, part):
    key = jax.random.fold_in(key, 5)
    key_rate, key_mark, key_whole, key_cut = jax.random.split(key, 4)
    rates = jax.random.randint(key_rate, (ROWS, 1), 3, 11)
    marks = jax.random.randint(key_mark, (ROWS, ROW_LEN), 0, 4096)
    starts = jnp.bitwise_and(marks, jnp.left_shift(1, rates) - 1) == 0
    column = jnp.arange(ROW_LEN, dtype=jnp.int32)[None, :]
    whole_row = jax.random.randint(key_whole, (), 0, ROWS)
    cut_at = jax.random.randint(key_cut, (), 0, GROUP)
    chosen = jnp.arange(ROWS, dtype=jnp.int32)[:, None] == whole_row
    starts = jnp.where(chosen, column == cut_at, starts)
    starts = starts | (column == 0)
    begins = lax.cummax(jnp.where(starts, column, 0), axis=1)
    return (column - begins).astype(jnp.int32)


def raised(drawn, rng, source, target, shards_of, factor):
    owner, partner = [(jnp.arange(drawn.shape[position]) // (drawn.shape[position] // shards_of)).reshape([-1 if axis == position else 1 for axis in range(drawn.ndim)]) for position in (source, target)]
    chosen = jax.random.permutation(rng, shards_of)[partner]
    strong = (owner == chosen) | (owner == (partner + shards_of // 2) % shards_of)
    return jnp.where(strong, factor * drawn, drawn)


def shard_levels(key, extent, pieces, low, high):
    factor_of = 1.0
    for dim, blocks in pieces:
        heights = jax.random.uniform(jax.random.fold_in(jax.random.fold_in(key, 6), dim), (blocks,), jnp.float32, low / len(pieces), high / len(pieces))
        factor_of = factor_of * jnp.repeat(jnp.exp(heights), extent[dim] // blocks).reshape((-1,) + (1,) * (len(extent) - 1 - dim))
    return factor_of


def gaussian(stream_key, shape, spread, bound, shards=(), held_as=jnp.bfloat16):
    array = jax.random.normal(stream_key, shape, jnp.float32) * spread
    if len(shards) > 0:
        array = shard_levels(stream_key, shape, shards, -0.22, 0.18) * array
    return jnp.clip(array, min=-bound, max=bound).astype(held_as)


def bell_draw_with(stream_key, extent, width, bound, cuts, heavy, kind=jnp.bfloat16):
    array = width * jax.random.normal(stream_key, extent, jnp.float32)
    if cuts:
        array = array * shard_levels(stream_key, extent, cuts, -0.22, 0.18)
    return jnp.clip(raised(array, jax.random.fold_in(stream_key, 3), *heavy), -bound, bound).astype(kind)


def setup_inputs(seed: int = 0) -> dict:
    keys = jax.random.split(jax.random.key(seed), 13)
    tokens = gaussian(keys[0], (ROWS, ROW_LEN, D), 1.0, 6.0, ((1, 8),))
    positions = draw_positions(jax.random.fold_in(keys[12], 71), 0)
    w_query = gaussian(keys[2], (D, HEADS * HEAD), (D // 2) ** -0.5, 0.1875, ((1, 4),))
    w_key = gaussian(keys[3], (D, HEADS * HEAD), (D // 2) ** -0.5, 0.1875, ((1, 4),))
    w_value = gaussian(keys[4], (D, HEADS * HEAD), D ** -0.5, 0.125, ((1, 4),))
    w_out = gaussian(keys[5], (HEADS * HEAD, D), (HEADS * HEAD // 16) ** -0.5, 0.5, ((0, 4),))
    w_gate = gaussian(keys[6], (D, FF), D ** -0.5, 0.125, ((1, 4),))
    w_up = gaussian(keys[7], (D, FF), D ** -0.5, 0.125, ((1, 4),))
    w_down = gaussian(keys[8], (FF, D), (FF // 4) ** -0.5, 0.15625, ((0, 4),))
    gain_attn = jnp.clip(1.0 + 0.1 * jax.random.normal(keys[9], (D,), jnp.float32), 0.5, 1.5)
    gain_ffn = jnp.clip(1.0 + 0.1 * jax.random.normal(keys[10], (D,), jnp.float32), 0.5, 1.5)
    cotangent = bell_draw_with(keys[11], (ROWS, ROW_LEN, D), 1.0, 6.0, ((1, 8),), (1, 2, 8, 2.0))
    return {"tokens": tokens, "positions": positions, "w_query": w_query, "w_key": w_key, "w_value": w_value, "w_out": w_out, "w_gate": w_gate, "w_up": w_up, "w_down": w_down, "gain_attn": gain_attn, "gain_ffn": gain_ffn, "cotangent": cotangent}


EPS = 1e-05
THETA = 10000.0
NEG = -1e+30

@jax.custom_vjp
def low(v):
    return lax.optimization_barrier(v.astype(jnp.bfloat16)).astype(jnp.float32)

@jax.custom_vjp
def low_back(v):
    return v

def low_keep(v):
    return (low(v), None)

def low_pass(kept, grad):
    return (grad,)

def back_keep(v):
    return (v, None)

def back_low(kept, grad):
    return (low(grad),)
low.defvjp(low_keep, low_pass)
low_back.defvjp(back_keep, back_low)

def rms_norm(inputs, gain_vec):
    return inputs * lax.rsqrt(lax.optimization_barrier(jnp.mean(inputs * inputs, axis=-1, keepdims=True)) + EPS) * gain_vec

def rotate(vectors, positions):
    half_size = vectors.shape[-1] // 2
    freq_table = THETA ** (-jnp.arange(half_size, dtype=jnp.float32) / half_size)
    angles = positions.astype(jnp.float32)[:, :, None, None] * freq_table
    cosine = jnp.cos(angles)
    sine_part = jnp.sin(angles)
    first_half = vectors[..., :half_size]
    second_half = vectors[..., half_size:]
    return jnp.concatenate([first_half * cosine - second_half * sine_part, second_half * cosine + first_half * sine_part], axis=-1)

def row_attention(row_parts):
    queries, keys_row, values_row, positions = row_parts
    block_len = min(512, ROW_LEN)
    padding = jnp.zeros((WINDOW,) + keys_row.shape[1:], jnp.float32)
    keys_pad = jnp.concatenate([padding, keys_row], axis=0)
    values_pad = jnp.concatenate([padding, values_row], axis=0)
    offset = jnp.arange(block_len, dtype=jnp.int32)[:, None] - jnp.arange(block_len + WINDOW, dtype=jnp.int32)[None, :] + WINDOW

    def one_block(block_index):
        start_at = (block_index * block_len).astype(jnp.int32)
        block_query = lax.dynamic_slice_in_dim(queries, start_at, block_len, 0)
        block_pos = lax.dynamic_slice_in_dim(positions, start_at, block_len, 0)
        block_key = lax.dynamic_slice_in_dim(keys_pad, start_at, block_len + WINDOW, 0)
        block_value = lax.dynamic_slice_in_dim(values_pad, start_at, block_len + WINDOW, 0)
        raw_scores = low_back(jnp.einsum('qhd,khd->hqk', block_query, block_key, precision=lax.Precision.HIGHEST) * HEAD ** (-0.5))
        visible = (offset >= 0) & (offset < WINDOW) & (offset <= block_pos[:, None])
        masked = jnp.where(visible[None], raw_scores, NEG)
        weights = low(jax.nn.softmax(masked, axis=-1))
        return jnp.einsum('hqk,khd->qhd', weights, block_value, precision=lax.Precision.HIGHEST)
    blocks = lax.map(jax.checkpoint(one_block), jnp.arange(ROW_LEN // block_len, dtype=jnp.int32))
    return blocks.reshape(queries.shape)

def layer_forward(inputs, w_query, w_key, w_value, w_out, w_gate, w_up, w_down, gain_attn, gain_ffn, positions):
    highest = lax.Precision.HIGHEST
    normed_attn = low(rms_norm(inputs, gain_attn))

    def project(weight):
        return jnp.einsum('rtd,de->rte', normed_attn, weight, precision=highest)
    head_shape = (ROWS, ROW_LEN, HEADS, HEAD)
    queries = low(rotate(low_back(project(w_query)).reshape(head_shape), positions))
    keys_all = low(rotate(low_back(project(w_key)).reshape(head_shape), positions))
    values_all = low(low_back(project(w_value))).reshape(head_shape)
    mixed_heads = lax.map(jax.checkpoint(row_attention), (queries, keys_all, values_all, positions))
    mixed_heads = low(low_back(mixed_heads.reshape(ROWS, ROW_LEN, HEADS * HEAD)))
    residual = inputs + low_back(jnp.einsum('rte,ed->rtd', mixed_heads, w_out, precision=highest))
    normed_ffn = low(rms_norm(residual, gain_ffn))
    gate_in = low_back(jnp.einsum('rtd,df->rtf', normed_ffn, w_gate, precision=highest))
    upward = low_back(jnp.einsum('rtd,df->rtf', normed_ffn, w_up, precision=highest))
    activated = low(jax.nn.silu(gate_in) * upward)
    return residual + low_back(jnp.einsum('rtf,fd->rtd', activated, w_down, precision=highest))

def reference(tokens, positions, w_query, w_key, w_value, w_out, w_gate, w_up, w_down, gain_attn, gain_ffn, cotangent):
    floats = tuple((argument.astype(jnp.float32) for argument in (tokens, w_query, w_key, w_value, w_out, w_gate, w_up, w_down, gain_attn, gain_ffn)))

    def forward_fixed(*members):
        return layer_forward(*members, positions)
    output, pullback = jax.vjp(forward_fixed, *floats)
    grads = pullback(cotangent.astype(jnp.float32))
    return (output.astype(jnp.bfloat16), grads[0].astype(jnp.bfloat16), grads[1], grads[2], grads[3], grads[4], grads[5], grads[6], grads[7], grads[8], grads[9])
```

```python
import functools
import math

import jax
import jax.numpy as jnp
from jax import lax
from jax.experimental import pallas as pl
from jax.experimental.pallas import tpu as pltpu
from jax.sharding import PartitionSpec as P

HEAD = 128
WINDOW = 1024
EPS = 1e-05
THETA = 10000.0
NEG = -1e30
LOG2E = 1.4426950408889634
BF16 = jnp.bfloat16
F32 = jnp.float32


def tp_send(x, mask):
    peers = lax.axis_size("tp")
    return lax.ppermute(x, "tp", [(i, i ^ mask) for i in range(peers)])


def seq_shift(x, by):
    peers = lax.axis_size("seq")
    return lax.ppermute(x, "seq", [(i, i + by) for i in range(peers) if 0 <= i + by < peers])


def core_swap(x):
    peers = lax.axis_size("seq")
    return lax.ppermute(x, "seq", [(i, i ^ 1) for i in range(peers)])


def chip_step(x, by, active):
    pairs = [(2 * c + k, 2 * (c + by) + k) for c in active for k in range(2)]
    return lax.ppermute(x, "seq", pairs)


def halo(x, reach, sign):
    spans = [x]
    core = lax.axis_index("seq") % 2
    if lax.axis_size("seq") % 2 or reach % 2:
        return spans + [seq_shift(x, sign * d) for d in range(1, reach + 1)]
    sender = 0 if sign > 0 else 1
    for _ in range(reach // 2):
        near = spans[-1]
        far = seq_shift(near, 2 * sign)
        between = core_swap(jnp.where(core == sender, near, far))
        spans += [between, far]
    return spans


def small_halo(x, reach, sign):
    return [x] + [seq_shift(x, sign * d) for d in range(1, reach + 1)]


def tp_gather(x):
    peers = lax.axis_size("tp")
    if peers != 4:
        return [x] + [tp_send(x, m) for m in range(1, peers)]
    half = x.shape[0] // 2
    a, b = x[:half], x[half:]
    a_x = tp_send(a, 1)
    b_y = tp_send(b, 2)
    a_y = tp_send(a, 2)
    b_x = tp_send(b, 1)
    a_xy = tp_send(a_x, 2)
    b_xy = tp_send(b_y, 1)
    join = lambda u, v: jnp.concatenate([u, v], axis=0)
    return [x, join(a_x, b_x), join(a_y, b_y), join(a_xy, b_xy)]


def tp_reduce(part):
    pieces = part
    peers = lax.axis_size("tp")
    rows = pieces.shape[0] // peers
    piece = lambda m: pieces[m * rows : (m + 1) * rows]
    if peers != 4:
        total = piece(0).astype(F32)
        for m in range(1, peers):
            total = total + tp_send(piece(m), m).astype(F32)
        return total
    half = rows // 2
    top = lambda m: pieces[m * rows : m * rows + half]
    low = lambda m: pieces[m * rows + half : (m + 1) * rows]
    a3 = tp_send(top(3), 1)
    b3 = tp_send(low(3), 2)
    a1 = tp_send(top(1), 1)
    b2 = tp_send(low(2), 2)
    a2 = tp_send((top(2).astype(F32) + a3.astype(F32)).astype(BF16), 2)
    b1 = tp_send((low(1).astype(F32) + b3.astype(F32)).astype(BF16), 1)
    upper = top(0).astype(F32) + a1.astype(F32) + a2.astype(F32)
    lower = low(0).astype(F32) + b2.astype(F32) + b1.astype(F32)
    return jnp.concatenate([upper, lower], axis=0)


def place(pieces):
    peers = len(pieces)
    t = lax.axis_index("tp")
    rows, width = pieces[0].shape
    out = jnp.zeros((peers * rows, width), pieces[0].dtype)
    for m, piece in enumerate(pieces):
        out = lax.dynamic_update_slice(out, piece, ((t ^ m) * rows, 0))
    return out


def seq_total(half_of, axis):
    chips = lax.axis_size("seq") // 2
    s = lax.axis_index("seq")
    k, c = s % 2, s // 2
    from_core = core_swap(half_of(1 - k).astype(BF16))
    acc = (half_of(k) + from_core.astype(F32)).astype(BF16)
    width = acc.shape[axis] // chips
    shard = lambda i: lax.dynamic_slice_in_dim(acc, i * width, width, axis)
    right = left = None
    for step in range(1, chips):
        send_r = shard(jnp.clip(chips - step + c, 0, chips - 1))
        send_l = shard(jnp.clip(c + step - chips, 0, chips - 1))
        if step > 1:
            send_r = (send_r.astype(F32) + right.astype(F32)).astype(BF16)
            send_l = (send_l.astype(F32) + left.astype(F32)).astype(BF16)
        right = chip_step(send_r, 1, range(0, step))
        left = chip_step(send_l, -1, range(chips - step, chips))
    own = (shard(c).astype(F32) + right.astype(F32) + left.astype(F32)).astype(BF16)
    before, after = [], []
    cur_r = cur_l = own
    for step in range(1, chips):
        cur_r = chip_step(cur_r, 1, range(step - 1, chips - 1))
        cur_l = chip_step(cur_l, -1, range(1, chips - step + 1))
        before.insert(0, cur_r)
        after.append(cur_l)
    line = jnp.concatenate(before + [own] + after, axis=axis)
    mine = lax.dynamic_slice_in_dim(line, (chips - 1 - c) * width, chips * width, axis)
    theirs = core_swap(mine)
    first = jnp.where(k == 0, mine, theirs).astype(F32)
    second = jnp.where(k == 0, theirs, mine).astype(F32)
    return jnp.concatenate([first, second], axis=axis)


def dot_tt(a, b):
    return lax.dot_general(a, b, (((1,), (1,)), ((), ())), preferred_element_type=F32)


def dot_nn(a, b):
    return lax.dot_general(a, b, (((1,), (0,)), ((), ())), preferred_element_type=F32)


def swap_lanes(x):
    half = x.shape[-1] // 2
    return jnp.concatenate([x[:, half:], x[:, :half]], axis=-1)


def attend_kernel(reach, low_ref, q_ref, *refs):
    k_refs, v_refs = refs[: reach + 1], refs[reach + 1 : 2 * reach + 2]
    out_ref, lse_ref = refs[2 * reach + 2 :]
    span = q_ref.shape[0]
    c = HEAD ** (-0.5) * LOG2E
    q = q_ref[...]
    low = low_ref[...]
    key = lax.broadcasted_iota(jnp.int32, (span, span), 1)
    scores = []
    for d in range(reach + 1):
        s = dot_tt(q, k_refs[d][...])
        seen = key >= low + d * span
        if d == 0:
            seen = seen & (key <= lax.broadcasted_iota(jnp.int32, (span, span), 0))
        scores.append(jnp.where(seen, s, NEG))
    top = functools.reduce(jnp.maximum, scores)
    top = jnp.max(top, axis=-1, keepdims=True)
    total = jnp.zeros((span, span), F32)
    mixed = jnp.zeros((span, HEAD), F32)
    for d in range(reach + 1):
        e = jnp.exp2((scores[d] - top) * c)
        total = total + e
        mixed = mixed + dot_nn(e.astype(BF16), v_refs[d][...])
    total = jnp.sum(total, axis=-1, keepdims=True)
    out_ref[...] = (mixed / total).astype(BF16)
    lse = top * c + jnp.log2(total)
    lse_ref[...] = jnp.transpose(jnp.broadcast_to(lse, (span, 128)))[:1][None, None]


def attend(queries, spans, low_col, rows):
    tokens, flat = queries.shape
    reach = len(spans) - 1
    heads = flat // HEAD
    span = tokens // rows
    head_spec = pl.BlockSpec((span, HEAD), lambda r, h: (r, h))
    value_spec = pl.BlockSpec((span, HEAD), lambda r, h: (r, heads + h))
    pairs = rows * heads * span * span * (reach + 1)
    return pl.pallas_call(
        functools.partial(attend_kernel, reach),
        grid=(rows, heads),
        in_specs=[pl.BlockSpec((span, 1), lambda r, h: (r, 0)), head_spec]
        + [head_spec] * (reach + 1)
        + [value_spec] * (reach + 1),
        out_specs=[head_spec, pl.BlockSpec((1, 1, 1, span), lambda r, h: (r, h, 0, 0))],
        out_shape=[
            jax.ShapeDtypeStruct((tokens, flat), BF16),
            jax.ShapeDtypeStruct((rows, heads, 1, span), F32),
        ],
        compiler_params=pltpu.CompilerParams(vmem_limit_bytes=48 * 1024 * 1024),
        cost_estimate=pl.CostEstimate(
            flops=8 * pairs * HEAD, bytes_accessed=16 * 1024 * 1024, transcendentals=pairs
        ),
        name="attend",
    )(low_col, queries, *spans, *spans)


def query_back_kernel(reach, low_ref, cos_ref, sin_ref, lse_ref, q_ref, g_ref, o_ref, *refs):
    k_refs, v_refs = refs[: reach + 1], refs[reach + 1 : 2 * reach + 2]
    (out_ref,) = refs[2 * reach + 2 :]
    span = q_ref.shape[0]
    c = HEAD ** (-0.5) * LOG2E
    q = q_ref[...]
    g = g_ref[...]
    low = low_ref[...]
    lse = jnp.transpose(jnp.broadcast_to(lse_ref[0, 0], (128, span)))[:, :1]
    delta = jnp.sum(g.astype(F32) * o_ref[...].astype(F32), axis=-1, keepdims=True)
    key = lax.broadcasted_iota(jnp.int32, (span, span), 1)
    grad = jnp.zeros((span, HEAD), F32)
    for d in range(reach + 1):
        keys = k_refs[d][...]
        s = dot_tt(q, keys)
        seen = key >= low + d * span
        if d == 0:
            seen = seen & (key <= lax.broadcasted_iota(jnp.int32, (span, span), 0))
        p = jnp.where(seen, jnp.exp2(s * c - lse), 0.0)
        dp = dot_tt(g, v_refs[d][...])
        ds = (p * (dp - delta)).astype(BF16)
        grad = grad + dot_nn(ds, keys)
    grad = grad * HEAD ** (-0.5)
    out_ref[...] = (grad * cos_ref[...] + swap_lanes(grad * sin_ref[...])).astype(BF16)


def query_back(queries, mixed_grad, mixed, spans, lse, low_col, tables, rows):
    tokens, flat = queries.shape
    reach = len(spans) - 1
    heads = flat // HEAD
    span = tokens // rows
    head_spec = pl.BlockSpec((span, HEAD), lambda r, h: (r, h))
    value_spec = pl.BlockSpec((span, HEAD), lambda r, h: (r, heads + h))
    table_spec = pl.BlockSpec((span, HEAD), lambda r, h: (r, 0))
    pairs = rows * heads * span * span * (reach + 1)
    return pl.pallas_call(
        functools.partial(query_back_kernel, reach),
        grid=(rows, heads),
        in_specs=[
            pl.BlockSpec((span, 1), lambda r, h: (r, 0)),
            table_spec,
            table_spec,
            pl.BlockSpec((1, 1, 1, span), lambda r, h: (r, h, 0, 0)),
            head_spec,
            head_spec,
            head_spec,
        ]
        + [head_spec] * (reach + 1)
        + [value_spec] * (reach + 1),
        out_specs=head_spec,
        out_shape=jax.ShapeDtypeStruct((tokens, flat), BF16),
        compiler_params=pltpu.CompilerParams(vmem_limit_bytes=48 * 1024 * 1024),
        cost_estimate=pl.CostEstimate(
            flops=12 * pairs * HEAD, bytes_accessed=20 * 1024 * 1024, transcendentals=pairs
        ),
        name="query_back",
    )(low_col, *tables, lse, queries, mixed_grad, mixed, *spans, *spans)


def key_back_kernel(reach, cos_ref, sin_ref, k_ref, v_ref, *refs):
    n = reach + 1
    low_refs, lse_refs, delta_refs, q_refs, g_refs = [refs[i * n : (i + 1) * n] for i in range(5)]
    key_out, value_out = refs[5 * n :]
    span = k_ref.shape[0]
    c = HEAD ** (-0.5) * LOG2E
    keys = k_ref[...]
    values = v_ref[...]
    key = lax.broadcasted_iota(jnp.int32, (span, span), 0)
    key_grad = jnp.zeros((span, HEAD), F32)
    value_grad = jnp.zeros((span, HEAD), F32)
    for d in range(n):
        q = q_refs[d][...]
        g = g_refs[d][...]
        s = dot_tt(keys, q)
        seen = key >= low_refs[d][0] + d * span
        if d == 0:
            seen = seen & (key <= lax.broadcasted_iota(jnp.int32, (span, span), 1))
        p = jnp.where(seen, jnp.exp2(s * c - lse_refs[d][0, 0]), 0.0)
        value_grad = value_grad + dot_nn(p.astype(BF16), g)
        dp = dot_tt(values, g)
        ds = (p * (dp - delta_refs[d][0, 0])).astype(BF16)
        key_grad = key_grad + dot_nn(ds, q)
    key_grad = key_grad * HEAD ** (-0.5)
    key_out[...] = (key_grad * cos_ref[...] + swap_lanes(key_grad * sin_ref[...])).astype(BF16)
    value_out[...] = value_grad.astype(BF16)


def key_back(pair, lows, lses, deltas, queries, grads, tables, rows):
    tokens, flat = queries[0].shape
    n = len(queries)
    heads = flat // HEAD
    span = tokens // rows
    head_spec = pl.BlockSpec((span, HEAD), lambda r, h: (r, h))
    value_spec = pl.BlockSpec((span, HEAD), lambda r, h: (r, heads + h))
    table_spec = pl.BlockSpec((span, HEAD), lambda r, h: (r, 0))
    low_spec = pl.BlockSpec((1, 1, span), lambda r, h: (r, 0, 0))
    stat_spec = pl.BlockSpec((1, 1, 1, span), lambda r, h: (r, h, 0, 0))
    pairs = rows * heads * span * span * n
    return pl.pallas_call(
        functools.partial(key_back_kernel, n - 1),
        grid=(rows, heads),
        in_specs=[table_spec, table_spec, head_spec, value_spec]
        + [low_spec] * n
        + [stat_spec] * (2 * n)
        + [head_spec] * (2 * n),
        out_specs=[head_spec, head_spec],
        out_shape=[jax.ShapeDtypeStruct((tokens, flat), BF16)] * 2,
        compiler_params=pltpu.CompilerParams(vmem_limit_bytes=48 * 1024 * 1024),
        cost_estimate=pl.CostEstimate(
            flops=16 * pairs * HEAD, bytes_accessed=20 * 1024 * 1024, transcendentals=pairs
        ),
        name="key_back",
    )(*tables, pair, pair, *lows, *lses, *deltas, *queries, *grads)


def across(left_side, right_side):
    return lax.dot_general(
        left_side, right_side, (((0,), (0,)), ((), ())), preferred_element_type=F32
    )


def against(left_side, right_side):
    return dot_tt(left_side, right_side)


def inverse_rms(v):
    return lax.rsqrt(jnp.mean(v * v, axis=-1, keepdims=True) + EPS)


def norm_backward(upstream, inputs, inverse, gain_vec):
    plain_norm = inputs * inverse
    scaled = upstream * gain_vec
    inner_mean = jnp.mean(scaled * plain_norm, axis=-1, keepdims=True)
    return (inverse * (scaled - plain_norm * inner_mean), jnp.sum(upstream * plain_norm, axis=0))


def half_columns(x, k):
    width = x.shape[1] // 2
    return lax.dynamic_slice_in_dim(x, k * width, width, 1)


def per_device(
    tokens,
    positions,
    w_query,
    w_key,
    w_value,
    w_out,
    w_gate,
    w_up,
    w_down,
    gain_attn,
    gain_ffn,
    cotangent,
):
    rows, span, width = tokens.shape
    count = rows * span
    peers = lax.axis_size("tp")
    own = count // peers
    t = lax.axis_index("tp")
    reach = WINDOW // span
    flat = w_query.shape[1]
    heads = flat // HEAD

    def reorder(x):
        parts = x.reshape((peers, rows // peers) + x.shape[1:])
        picked = [lax.dynamic_index_in_dim(parts, t ^ m, 0, keepdims=False) for m in range(peers)]
        return jnp.concatenate(picked, axis=0)

    out_rows = [w_out] + [tp_send(w_out, m) for m in range(1, peers)]

    place_of = reorder(positions)
    within = jnp.arange(span, dtype=jnp.int32)[None, :]
    low = jnp.maximum(within - place_of, within - (WINDOW - 1))
    low_col = low.reshape(count, 1)
    lows = small_halo(low.reshape(rows, 1, span), reach, -1)

    half_size = HEAD // 2
    freq = THETA ** (-jnp.arange(half_size, dtype=F32) / half_size)
    angles = place_of.reshape(count, 1).astype(F32) * freq
    cosine, sine = jnp.cos(angles), jnp.sin(angles)
    tables = (
        jnp.concatenate([cosine, cosine], axis=-1),
        jnp.concatenate([-sine, sine], axis=-1),
    )

    def rotate(lin):
        vectors = lin.reshape(count, heads, HEAD)
        swapped = jnp.concatenate([vectors[..., half_size:], vectors[..., :half_size]], axis=-1)
        return (vectors * tables[0][:, None] + swapped * tables[1][:, None]).reshape(count, flat)

    tok = reorder(tokens).reshape(count, width).astype(F32)
    normed_attn = (tok * inverse_rms(tok) * gain_attn).astype(BF16)
    tok_own = tok[:own]

    pair = jnp.concatenate(
        [rotate(dot_nn(normed_attn, w_key)), dot_nn(normed_attn, w_value)], axis=1
    ).astype(BF16)
    spans = halo(pair, reach, 1)
    queries = rotate(dot_nn(normed_attn, w_query)).astype(BF16)
    later_queries = halo(queries, reach, -1)

    upstream_low = reorder(cotangent).reshape(count, width)
    act_grad = against(upstream_low, w_down)

    mixed, lse = attend(queries, spans, low_col, rows)
    lses = small_halo(lse, reach, -1)

    mixed_own = [mixed[:own]]
    mixed_own += [tp_send(mixed[m * own : (m + 1) * own], m) for m in range(1, peers)]
    residual = tok_own
    for m in range(peers):
        residual = residual + dot_nn(mixed_own[m], out_rows[m])
    inverse_ffn = inverse_rms(residual)
    normed_own = (residual * inverse_ffn * gain_ffn).astype(BF16)
    normed_ffn = jnp.concatenate(tp_gather(normed_own), axis=0)

    gate_in = dot_nn(normed_ffn, w_gate)
    upward = dot_nn(normed_ffn, w_up)
    sigmoid_gate = jax.nn.sigmoid(gate_in)
    swish_gate = gate_in * sigmoid_gate
    activated = (swish_gate * upward).astype(BF16)
    gate_grad = (
        act_grad * upward * (sigmoid_gate * (1.0 + gate_in * (1.0 - sigmoid_gate)))
    ).astype(BF16)
    up_grad = (act_grad * swish_gate).astype(BF16)

    full_down = seq_total(lambda k: across(activated, half_columns(upstream_low, k)), 1)

    ffn_back = (against(gate_grad, w_gate) + against(up_grad, w_up)).astype(BF16)
    ffn_back = tp_reduce(ffn_back)
    back_norm, gain_ffn_grad = norm_backward(ffn_back, residual, inverse_ffn, gain_ffn)
    upstream_own = upstream_low[:own].astype(F32)
    resid_grad = upstream_own + back_norm
    resid_low = resid_grad.astype(BF16)

    grads_own = [against(resid_low, out_rows[m]).astype(BF16) for m in range(peers)]
    mixed_grad = jnp.concatenate(
        [grads_own[0]] + [tp_send(grads_own[m], m) for m in range(1, peers)], axis=0
    )
    later_grads = halo(mixed_grad, reach, -1)
    delta = jnp.sum(
        (mixed_grad.astype(F32) * mixed.astype(F32)).reshape(rows, span, heads, HEAD), axis=-1
    )
    delta = jnp.transpose(delta, (0, 2, 1)).reshape(rows, heads, 1, span)
    deltas = small_halo(delta, reach, -1)

    full_gate = seq_total(lambda k: across(half_columns(normed_ffn, k), gate_grad), 0)
    full_up = seq_total(lambda k: across(half_columns(normed_ffn, k), up_grad), 0)

    ffn_part = dot_nn(activated, w_down).astype(BF16)
    output = (residual + tp_reduce(ffn_part)).astype(BF16)
    output = place(tp_gather(output))

    resid_all = jnp.concatenate(tp_gather(resid_low), axis=0)

    query_grad = query_back(queries, mixed_grad, mixed, spans, lse, low_col, tables, rows)
    key_grad, value_grad = key_back(
        pair, lows, lses, deltas, later_queries, later_grads, tables, rows
    )

    full_out = seq_total(lambda k: across(half_columns(mixed, k), resid_all), 0)
    full_query = seq_total(lambda k: across(half_columns(normed_attn, k), query_grad), 0)
    full_key = seq_total(lambda k: across(half_columns(normed_attn, k), key_grad), 0)
    full_value = seq_total(lambda k: across(half_columns(normed_attn, k), value_grad), 0)

    attn_back = (
        against(query_grad, w_query) + against(key_grad, w_key) + against(value_grad, w_value)
    ).astype(BF16)
    attn_back = tp_reduce(attn_back)
    back_norm, gain_attn_grad = norm_backward(
        attn_back, tok_own, inverse_rms(tok_own), gain_attn
    )
    token_grad = place(tp_gather((resid_grad + back_norm).astype(BF16)))

    gain_grads = lax.psum(jnp.stack([gain_attn_grad, gain_ffn_grad]), ("seq", "tp"))
    return (
        output.reshape(rows, span, width),
        token_grad.reshape(rows, span, width),
        full_query,
        full_key,
        full_value,
        full_out,
        full_gate,
        full_up,
        full_down,
        gain_grads[0],
        gain_grads[1],
    )


def solution(mesh):
    return jax.shard_map(
        per_device,
        mesh=mesh,
        in_specs=(
            P(None, "seq", None),
            P(None, "seq"),
            P(None, "tp"),
            P(None, "tp"),
            P(None, "tp"),
            P("tp", None),
            P(None, "tp"),
            P(None, "tp"),
            P("tp", None),
            P(),
            P(),
            P(None, "seq", None),
        ),
        out_specs=(
            P(None, "seq", None),
            P(None, "seq", None),
            P(None, "tp"),
            P(None, "tp"),
            P(None, "tp"),
            P("tp", None),
            P(None, "tp"),
            P(None, "tp"),
            P("tp", None),
            P(),
            P(),
        ),
        check_vma=False,
    )
```

```python
import functools

import jax
import jax.numpy as jnp
from jax import lax
from jax.experimental import pallas as pl
from jax.experimental.pallas import tpu as pltpu
from jax.sharding import PartitionSpec as P

HEAD = 128
WINDOW = 1024
EPS = 1e-05
THETA = 10000.0
NEG = -1e30
LOG2E = 1.4426950408889634
CHUNKS = 2
BF16 = jnp.bfloat16
F32 = jnp.float32
VMEM_LIMIT = 48 * 1024 * 1024


def cost(us):
    return pl.CostEstimate(flops=0, bytes_accessed=int(us * 0.5 * 3.69e6), transcendentals=0)


class Order:
    def __init__(self):
        self.last = ()

    def gate(self, *arrays):
        tied = lax.optimization_barrier(tuple(arrays) + tuple(self.last))[: len(arrays)]
        return tied[0] if len(arrays) == 1 else tied

    def mark(self, *arrays):
        self.last = arrays


def tp_send(x, mask):
    peers = lax.axis_size("tp")
    return lax.ppermute(x, "tp", [(i, i ^ mask) for i in range(peers)])


def seq_shift(x, by):
    peers = lax.axis_size("seq")
    return lax.ppermute(x, "seq", [(i, i + by) for i in range(peers) if 0 <= i + by < peers])


def core_swap(x):
    peers = lax.axis_size("seq")
    return lax.ppermute(x, "seq", [(i, i ^ 1) for i in range(peers)])


def chip_pairs(x, chip_pairs_list):
    pairs = [(2 * a + k, 2 * b + k) for a, b in chip_pairs_list for k in range(2)]
    return lax.ppermute(x, "seq", pairs)


def between_spans(near, far, sign):
    core = lax.axis_index("seq") % 2
    return core_swap(pick(core if sign > 0 else 1 - core, near, far))


def total_over_all(x):
    peers, chips = lax.axis_size("tp"), lax.axis_size("seq") // 2
    mask = 1
    while mask < peers:
        x = x + tp_send(x, mask)
        mask *= 2
    x = x + core_swap(x)
    c = lax.axis_index("seq") // 2
    mid = chips // 2 - 1
    for i in range(mid):
        x = x + chip_pairs(x, [(i, i + 1), (chips - 1 - i, chips - 2 - i)])
    x = x + chip_pairs(x, [(mid, mid + 1), (mid + 1, mid)])
    for j in range(mid, 0, -1):
        moved = chip_pairs(x, [(j, j - 1), (chips - 1 - j, chips - j)])
        x = jnp.where((c == j - 1) | (c == chips - j), moved, x)
    return x


def tp_gather(x):
    peers = lax.axis_size("tp")
    if peers != 4:
        return [x] + [tp_send(x, m) for m in range(1, peers)]
    half = x.shape[0] // 2
    x1 = tp_send(x, 1)
    x2 = tp_send(x, 2)
    return [x, x1, x2, tp_send(x1[:half], 2), tp_send(x2[half:], 1)]


class TpReduce:
    def __init__(self, parts):
        self.parts = parts
        self.peers = lax.axis_size("tp")
        if self.peers == 4:
            self.a = tp_send(parts[3], 1)
            self.b = tp_send(parts[4], 2)

    def second(self, order):
        parts = self.parts
        if self.peers == 4:
            a, b = order.gate(self.a, self.b)
            x, y = reduce_second(parts[1], parts[2], a, b)
            order.mark(x, y)
            self.got = [tp_send(x, 1), tp_send(y, 2)]
        else:
            self.got = [tp_send(parts[m], m) for m in range(1, self.peers)]

    def terms(self):
        return [self.parts[0]] + self.got


class LineSum:
    def __init__(self, order, left, right, axis, parts=1):
        self.order, self.left, self.right, self.axis, self.parts = order, left, right, axis, parts
        s = lax.axis_index("seq")
        self.k, self.c = s % 2, s // 2
        self.chips = lax.axis_size("seq") // 2
        self.stage = [0] * parts
        self.moved = [None] * parts

    def begin(self):
        left, right = self.order.gate(self.left, self.right)
        (sent,) = outer(left, right, 1 - self.k, self.axis, 1)
        self.order.mark(sent)
        self.swapped = core_swap(sent)

    def own(self):
        left, right, swapped = self.order.gate(self.left, self.right, self.swapped)
        self.acc = list(outer(left, right, self.k, self.axis, self.parts, swapped))
        self.order.mark(self.acc[0])

    def launch(self, j=0):
        self.acc[j] = self.order.gate(self.acc[j])
        self.send(j)

    def send(self, j):
        c = self.chips
        mid = c // 2 - 1
        i = self.stage[j]
        if i < mid:
            pairs = [(i, i + 1), (c - 1 - i, c - 2 - i)]
        elif i == mid:
            pairs = [(mid, mid + 1), (mid + 1, mid)]
        else:
            n = 2 * mid + 1 - i
            pairs = [(n, n - 1), (c - 1 - n, c - n)]
        self.takers = [b for _, b in pairs]
        self.moved[j] = chip_pairs(self.acc[j], pairs)

    def step(self, j=0):
        acc, moved = self.order.gate(self.acc[j], self.moved[j])
        mid = self.chips // 2 - 1
        i = self.stage[j]
        if i <= mid:
            acc = fold(acc, moved)
        else:
            n = 2 * mid + 1 - i
            taker = (self.c == n - 1) | (self.c == self.chips - n)
            acc = pick(taker.astype(jnp.int32), acc, moved)
        self.acc[j] = acc
        self.order.mark(acc)
        self.stage[j] += 1
        if self.stage[j] < self.chips - 1:
            self.send(j)
        else:
            self.moved[j] = core_swap(acc)

    def rest(self):
        for j in range(self.parts):
            while self.stage[j] < self.chips - 1:
                self.step(j)

    def finish(self):
        self.rest()
        arrays = self.order.gate(*self.acc, *self.moved)
        out = unite(arrays[: self.parts], arrays[self.parts :], self.k, self.axis)
        self.order.mark(out)
        return out


def dot_tt(a, b):
    return lax.dot_general(a, b, (((1,), (1,)), ((), ())), preferred_element_type=F32)


def dot_nn(a, b):
    return lax.dot_general(a, b, (((1,), (0,)), ((), ())), preferred_element_type=F32)


def swap_lanes(x):
    half = x.shape[-1] // 2
    return jnp.concatenate([x[:, half:], x[:, :half]], axis=-1)


def params():
    return pltpu.CompilerParams(vmem_limit_bytes=VMEM_LIMIT)


def project_kernel(turns, norm, x_ref, cos_ref, sin_ref, gain_ref, *refs):
    n = len(turns)
    w_refs, out_ref = refs[:n], refs[-1]
    x = x_ref[...]
    if norm:
        v = x.astype(F32)
        inverse = lax.rsqrt(jnp.mean(v * v, axis=-1, keepdims=True) + EPS)
        x = (v * inverse * gain_ref[...]).astype(BF16)
        refs[-2][...] = x
    cos, sin = cos_ref[...], sin_ref[...]
    at = 0
    for turn, w_ref in zip(turns, w_refs):
        lin = dot_nn(x, w_ref[...])
        for h in range(lin.shape[1] // HEAD):
            part = lin[:, h * HEAD : (h + 1) * HEAD]
            if turn:
                part = part * cos + swap_lanes(part) * sin
            out_ref[:, at : at + HEAD] = part.astype(BF16)
            at += HEAD


def project(x, tables, gain, weights, turns, first, count, norm=False, normed=None):
    total, width = x.shape
    flat = sum(w.shape[1] for w in weights)
    block = 256 if count % 256 == 0 else 128
    skip = first // block
    rows_of = lambda n: pl.BlockSpec((block, n), lambda i: (i + skip, 0))
    out_specs = [pl.BlockSpec((block, flat), lambda i: (i, 0))]
    out_shape = [jax.ShapeDtypeStruct((count, flat), BF16)]
    if norm:
        out_specs.insert(0, rows_of(width))
        out_shape.insert(0, jax.ShapeDtypeStruct(x.shape, BF16))
    kept = [] if normed is None else [normed]
    return pl.pallas_call(
        functools.partial(project_kernel, turns, norm),
        grid=(count // block,),
        in_specs=[rows_of(width), rows_of(HEAD), rows_of(HEAD)]
        + [pl.BlockSpec((1, width), lambda i: (0, 0))]
        + [pl.BlockSpec(w.shape, lambda i: (0, 0)) for w in weights]
        + [pl.BlockSpec(memory_space=pl.ANY)] * len(kept),
        out_specs=out_specs,
        out_shape=out_shape,
        input_output_aliases={4 + len(weights): 0} if kept else {},
        compiler_params=params(),
        cost_estimate=cost(6),
        name="project",
    )(x, *tables, gain.reshape(1, width), *weights, *kept)


def attend_kernel(reach, low_ref, q_ref, *refs):
    k_refs, v_refs = refs[: reach + 1], refs[reach + 1 : 2 * reach + 2]
    out_ref, lse_ref = refs[-2:]
    span = q_ref.shape[0]
    c = HEAD ** (-0.5) * LOG2E
    q = q_ref[...]
    low = low_ref[...]
    key = lax.broadcasted_iota(jnp.int32, (span, span), 1)
    scores = []
    for d in range(reach + 1):
        s = dot_tt(q, k_refs[d][...])
        seen = key >= low + d * span
        if d == 0:
            seen = seen & (key <= lax.broadcasted_iota(jnp.int32, (span, span), 0))
        scores.append(jnp.where(seen, s, NEG))
    top = functools.reduce(jnp.maximum, scores)
    top = jnp.max(top, axis=-1, keepdims=True)
    total = jnp.zeros((span, span), F32)
    mixed = jnp.zeros((span, HEAD), F32)
    for d in range(reach + 1):
        e = jnp.exp2((scores[d] - top) * c)
        total = total + e
        mixed = mixed + dot_nn(e.astype(BF16), v_refs[d][...])
    total = jnp.sum(total, axis=-1, keepdims=True)
    out_ref[...] = (mixed / total).astype(BF16)
    lse = top * c + jnp.log2(total)
    lse_ref[...] = jnp.transpose(jnp.broadcast_to(lse, (span, 128)))[:1][None, None]


def attend(queries, spans, low_col, rows, first, before):
    flat = queries.shape[1]
    tokens = spans[0].shape[0]
    reach = len(spans) - 1
    heads = flat // HEAD
    span = tokens // rows
    head_spec = pl.BlockSpec((span, HEAD), lambda r, h: (r, h))
    value_spec = pl.BlockSpec((span, HEAD), lambda r, h: (r, heads + h))
    pairs = rows * heads * span * span * (reach + 1)
    return pl.pallas_call(
        functools.partial(attend_kernel, reach),
        grid=(rows, heads),
        in_specs=[
            pl.BlockSpec((span, 1), lambda r, h: (r + first, 0)),
            pl.BlockSpec((span, HEAD), lambda r, h: (r + first, h)),
        ]
        + [head_spec] * (reach + 1)
        + [value_spec] * (reach + 1)
        + [pl.BlockSpec(memory_space=pl.ANY)] * len(before),
        out_specs=[
            pl.BlockSpec((span, HEAD), lambda r, h: (r + first, h)),
            pl.BlockSpec((1, 1, 1, span), lambda r, h: (r, h, 0, 0)),
        ],
        out_shape=[
            jax.ShapeDtypeStruct(queries.shape, BF16),
            jax.ShapeDtypeStruct((rows, heads, 1, span), F32),
        ],
        input_output_aliases={2 + 2 * (reach + 1): 0} if before else {},
        compiler_params=params(),
        cost_estimate=cost(9),
        name="attend",
    )(low_col, queries, *spans, *spans, *before)


def query_back_kernel(reach, low_ref, cos_ref, sin_ref, lse_ref, q_ref, g_ref, o_ref, *refs):
    k_refs, v_refs = refs[: reach + 1], refs[reach + 1 : 2 * reach + 2]
    out_ref = refs[-1]
    span = q_ref.shape[0]
    c = HEAD ** (-0.5) * LOG2E
    q = q_ref[...]
    g = g_ref[...]
    low = low_ref[...]
    lse = jnp.transpose(jnp.broadcast_to(lse_ref[0, 0], (128, span)))[:, :1]
    delta = jnp.sum(g.astype(F32) * o_ref[...].astype(F32), axis=-1, keepdims=True)
    key = lax.broadcasted_iota(jnp.int32, (span, span), 1)
    grad = jnp.zeros((span, HEAD), F32)
    for d in range(reach + 1):
        keys = k_refs[d][...]
        s = dot_tt(q, keys)
        seen = key >= low + d * span
        if d == 0:
            seen = seen & (key <= lax.broadcasted_iota(jnp.int32, (span, span), 0))
        p = jnp.where(seen, jnp.exp2(s * c - lse), 0.0)
        dp = dot_tt(g, v_refs[d][...])
        ds = (p * (dp - delta)).astype(BF16)
        grad = grad + dot_nn(ds, keys)
    grad = grad * HEAD ** (-0.5)
    out_ref[...] = (grad * cos_ref[...] + swap_lanes(grad * sin_ref[...])).astype(BF16)


def query_back(queries, mixed_grad, mixed, spans, lse, low_col, tables, rows, first, before):
    flat = queries.shape[1]
    tokens = spans[0].shape[0]
    reach = len(spans) - 1
    heads = flat // HEAD
    span = tokens // rows
    head_spec = pl.BlockSpec((span, HEAD), lambda r, h: (r, h))
    value_spec = pl.BlockSpec((span, HEAD), lambda r, h: (r, heads + h))
    whole_spec = pl.BlockSpec((span, HEAD), lambda r, h: (r + first, h))
    table_spec = pl.BlockSpec((span, HEAD), lambda r, h: (r + first, 0))
    return pl.pallas_call(
        functools.partial(query_back_kernel, reach),
        grid=(rows, heads),
        in_specs=[
            pl.BlockSpec((span, 1), lambda r, h: (r + first, 0)),
            table_spec,
            table_spec,
            pl.BlockSpec((1, 1, 1, span), lambda r, h: (r, h, 0, 0)),
            whole_spec,
            whole_spec,
            whole_spec,
        ]
        + [head_spec] * (reach + 1)
        + [value_spec] * (reach + 1)
        + [pl.BlockSpec(memory_space=pl.ANY)] * len(before),
        out_specs=whole_spec,
        out_shape=jax.ShapeDtypeStruct(queries.shape, BF16),
        input_output_aliases={7 + 2 * (reach + 1): 0} if before else {},
        compiler_params=params(),
        cost_estimate=cost(10),
        name="query_back",
    )(low_col, *tables, lse, queries, mixed_grad, mixed, *spans, *spans, *before)


def key_back_kernel(reach, cos_ref, sin_ref, k_ref, v_ref, *refs):
    n = reach + 1
    stat_refs, q_refs, g_refs = [refs[i * n : (i + 1) * n] for i in range(3)]
    key_out, value_out, stats = refs[-3:]
    span = k_ref.shape[0]
    c = HEAD ** (-0.5) * LOG2E
    h = pl.program_id(1)

    @pl.when(h == 0)
    def _():
        for d in range(n):
            block = stat_refs[d][...].astype(F32)
            per_row = block.shape[1] // span
            for index in range(1 + 2 * (block.shape[1] // HEAD)):
                total = jnp.zeros((1, span), F32)
                for third in range(3):
                    v = 3 * index + third
                    row, column = v // per_row, v % per_row * span
                    total = total + block[row : row + 1, column : column + span]
                stats[d, index] = total

    keys = k_ref[...]
    values = v_ref[...]
    key = lax.broadcasted_iota(jnp.int32, (span, span), 0)
    key_grad = jnp.zeros((span, HEAD), F32)
    value_grad = jnp.zeros((span, HEAD), F32)
    for d in range(n):
        low = stats[d, 0].astype(jnp.int32) + d * span
        q = q_refs[d][...]
        g = g_refs[d][...]
        s = dot_tt(keys, q)
        seen = key >= low
        if d == 0:
            seen = seen & (key <= lax.broadcasted_iota(jnp.int32, (span, span), 1))
        p = jnp.where(seen, jnp.exp2(s * c - stats[d, 1 + 2 * h]), 0.0)
        value_grad = value_grad + dot_nn(p.astype(BF16), g)
        dp = dot_tt(values, g)
        ds = (p * (dp - stats[d, 2 + 2 * h])).astype(BF16)
        key_grad = key_grad + dot_nn(ds, q)
    key_grad = key_grad * HEAD ** (-0.5)
    key_out[...] = (key_grad * cos_ref[...] + swap_lanes(key_grad * sin_ref[...])).astype(BF16)
    value_out[...] = value_grad.astype(BF16)


def key_back(pair, queries, grads, tables, rows, first, before):
    total, flat = queries[0].shape
    tokens = pair.shape[0]
    n = len(queries)
    heads = flat // HEAD
    span = tokens // rows
    head_spec = pl.BlockSpec((span, HEAD), lambda r, h: (r, h))
    value_spec = pl.BlockSpec((span, HEAD), lambda r, h: (r, heads + h))
    whole_spec = pl.BlockSpec((span, HEAD), lambda r, h: (r + first, h))
    table_spec = pl.BlockSpec((span, HEAD), lambda r, h: (r + first, 0))
    stats_at = total // STAT_ROWS + first
    stat_spec = pl.BlockSpec((STAT_ROWS, flat), lambda r, h: (r + stats_at, 0))
    return pl.pallas_call(
        functools.partial(key_back_kernel, n - 1),
        grid=(rows, heads),
        in_specs=[table_spec, table_spec, head_spec, value_spec]
        + [stat_spec] * n
        + [whole_spec] * (2 * n)
        + [pl.BlockSpec(memory_space=pl.ANY)] * len(before),
        out_specs=[whole_spec, whole_spec],
        out_shape=[jax.ShapeDtypeStruct((total, flat), BF16)] * 2,
        input_output_aliases={4 + 3 * n + i: i for i in range(len(before))},
        scratch_shapes=[pltpu.VMEM((n, 1 + 2 * heads, 1, span), F32)],
        compiler_params=params(),
        cost_estimate=cost(11),
        name="key_back",
    )(*tables, pair, pair, *grads, *queries, *grads, *before)


def residual_kernel(parts, tok_ref, gain_ref, *refs):
    x_refs, w_refs = refs[:parts], refs[parts : 2 * parts]
    res_ref, normed_ref = refs[2 * parts :]
    n = pl.program_id(0)
    tile = w_refs[0].shape[1]
    total = tok_ref[...].astype(F32)
    for x_ref, w_ref in zip(x_refs, w_refs):
        total = total + dot_nn(x_ref[...], w_ref[...])
    res_ref[:, pl.ds(pl.multiple_of(n * tile, tile), tile)] = total

    @pl.when(n == pl.num_programs(0) - 1)
    def _():
        v = res_ref[...]
        inverse = lax.rsqrt(jnp.mean(v * v, axis=-1, keepdims=True) + EPS)
        normed_ref[...] = (v * inverse * gain_ref[...]).astype(BF16)


def residual_of(tok, gain, pieces, weights):
    count, width = tok.shape
    tile = 512
    depth = weights[0].shape[0]
    whole = pl.BlockSpec((count, width), lambda n: (0, 0))
    return pl.pallas_call(
        functools.partial(residual_kernel, len(pieces)),
        grid=(width // tile,),
        in_specs=[
            pl.BlockSpec((count, tile), lambda n: (0, n)),
            pl.BlockSpec((1, width), lambda n: (0, 0)),
        ]
        + [pl.BlockSpec((count, depth), lambda n: (0, 0)) for _ in pieces]
        + [pl.BlockSpec((depth, tile), lambda n: (0, n)) for _ in weights],
        out_specs=[whole, whole],
        out_shape=[
            jax.ShapeDtypeStruct((count, width), F32),
            jax.ShapeDtypeStruct((count, width), BF16),
        ],
        compiler_params=params(),
        cost_estimate=cost(5),
        name="residual",
    )(tok, gain.reshape(1, width), *pieces, *weights)


def act_grad_kernel(pieces, t_ref, w_ref, *refs):
    cot_refs = refs[:pieces]
    upstream_ref, out_ref = refs[pieces:]
    part = cot_refs[0].shape[0]

    @pl.when(pl.program_id(0) == 0)
    def _():
        for j, cot_ref in enumerate(cot_refs):
            upstream_ref[j * part : (j + 1) * part] = cot_ref[...]

    out_ref[...] = dot_tt(upstream_ref[...], w_ref[...])


def act_grad_of(cot, w_down, t, peers):
    count, width = cot.shape
    hidden = w_down.shape[0]
    tile = 256
    pieces = CHUNKS * peers
    part = count // pieces
    near = lambda i, m: pl.BlockSpec((part, width), lambda n, t: (i * peers + (t[0] ^ m), 0))
    return pl.pallas_call(
        functools.partial(act_grad_kernel, pieces),
        grid_spec=pltpu.PrefetchScalarGridSpec(
            num_scalar_prefetch=1,
            grid=(pl.cdiv(hidden, tile),),
            in_specs=[pl.BlockSpec((tile, width), lambda n, t: (n, 0))]
            + [near(i, m) for i in range(CHUNKS) for m in range(peers)],
            out_specs=[
                pl.BlockSpec((count, width), lambda n, t: (0, 0)),
                pl.BlockSpec((count, tile), lambda n, t: (0, n)),
            ],
        ),
        out_shape=[
            jax.ShapeDtypeStruct((count, width), BF16),
            jax.ShapeDtypeStruct((count, hidden), F32),
        ],
        compiler_params=params(),
        cost_estimate=cost(12),
        name="act_grad",
    )(t, w_down, *[cot] * pieces)


def split_kernel(part, t_ref, x_ref, *out_refs):
    for m, out_ref in enumerate(out_refs):
        at = pl.multiple_of((t_ref[0] ^ m) * part, part)
        out_ref[...] = x_ref[pl.ds(at, part), :]


def split_near(x, t, peers, chunk):
    part = x.shape[0] // (peers * CHUNKS)
    whole = lambda shape: pl.BlockSpec(shape, lambda n, t: (0, 0))
    piece = (part, x.shape[1])
    return pl.pallas_call(
        functools.partial(split_kernel, part),
        grid_spec=pltpu.PrefetchScalarGridSpec(
            num_scalar_prefetch=1,
            grid=(1,),
            in_specs=[pl.BlockSpec((part * peers, x.shape[1]), lambda n, t: (chunk, 0))],
            out_specs=[whole(piece)] * peers,
        ),
        out_shape=[jax.ShapeDtypeStruct(piece, x.dtype)] * peers,
        compiler_params=params(),
        cost_estimate=cost(1.5),
        name="split_near",
    )(t, x)


STAT_ROWS = 16


def thirds(x):
    high = x.astype(BF16)
    rest = x - high.astype(F32)
    mid = rest.astype(BF16)
    return high, mid, (rest - mid.astype(F32)).astype(BF16)


def join_kernel(part, peers, t_ref, low_ref, *refs):
    piece_refs, mixed_ref, lse_refs = refs[:peers], refs[peers], refs[peers + 1 : -1]
    out_ref = refs[-1]
    for m, x_ref in enumerate(piece_refs):
        for i in range(CHUNKS):
            at = pl.multiple_of((i * peers + (t_ref[0] ^ m)) * part, part)
            out_ref[pl.ds(at, part), :] = x_ref[i * part : (i + 1) * part]
    rows, span = low_ref.shape[0], low_ref.shape[2]
    heads = lse_refs[0].shape[1]
    count = rows * span
    chunk_rows = rows // CHUNKS
    out_ref[count:] = jnp.zeros((out_ref.shape[0] - count, out_ref.shape[1]), BF16)
    for r in range(rows):
        i = r // chunk_rows
        g = out_ref[r * span : (r + 1) * span].astype(F32)
        product = g * mixed_ref[r * span : (r + 1) * span].astype(F32)
        vectors = [low_ref[r]]
        for h in range(heads):
            vectors.append(lse_refs[i][r % chunk_rows, h])
            delta = jnp.sum(product[:, h * HEAD : (h + 1) * HEAD], axis=-1, keepdims=True)
            vectors.append(jnp.transpose(jnp.broadcast_to(delta, (span, 128)))[:1])
        per_row = out_ref.shape[1] // span
        for v, x in enumerate([third for x in vectors for third in thirds(x)]):
            row, column = count + r * STAT_ROWS + v // per_row, v % per_row * span
            out_ref[row : row + 1, column : column + span] = x


def join_true(pieces, mixed, lses, low, t):
    peers = len(pieces)
    rows, width = pieces[0].shape
    extra = low.shape[0] * STAT_ROWS
    whole = lambda x: pl.BlockSpec(x.shape, lambda n, t: (0,) * x.ndim)
    out = jax.ShapeDtypeStruct((peers * rows + extra, width), BF16)
    return pl.pallas_call(
        functools.partial(join_kernel, rows // CHUNKS, peers),
        grid_spec=pltpu.PrefetchScalarGridSpec(
            num_scalar_prefetch=1,
            grid=(1,),
            in_specs=[whole(x) for x in (low, *pieces, mixed, *lses)],
            out_specs=whole(out),
        ),
        out_shape=out,
        compiler_params=params(),
        cost_estimate=cost(4),
        name="join_true",
    )(t, low, *pieces, mixed, *lses)


def ffn_kernel(pieces, act_grad_ref, gate_ref, up_ref, *refs):
    x_refs = refs[:pieces]
    x_ref, activated_ref, gate_grad_ref, up_grad_ref = refs[-4:]

    @pl.when(pl.program_id(0) == 0)
    def _():
        at = 0
        for piece_ref in x_refs:
            x_ref[at : at + piece_ref.shape[0]] = piece_ref[...]
            at += piece_ref.shape[0]

    x = x_ref[...]
    gate_in = dot_tt(x, gate_ref[...])
    upward = dot_tt(x, up_ref[...])
    act_grad = act_grad_ref[...]
    sigmoid_gate = jax.nn.sigmoid(gate_in)
    swish_gate = gate_in * sigmoid_gate
    activated_ref[...] = (swish_gate * upward).astype(BF16)
    gate_grad_ref[...] = (
        act_grad * upward * (sigmoid_gate * (1.0 + gate_in * (1.0 - sigmoid_gate)))
    ).astype(BF16)
    up_grad_ref[...] = (act_grad * swish_gate).astype(BF16)


def ffn(x_pieces, act_grad, gate_t, up_t, chunk, before):
    hidden, width = gate_t.shape
    count = sum(x.shape[0] for x in x_pieces)
    tile = 384
    weight = pl.BlockSpec((tile, width), lambda n: (n, 0))
    block = pl.BlockSpec((count, tile), lambda n: (chunk, n))
    out = jax.ShapeDtypeStruct((CHUNKS * count, hidden), BF16)
    kept = [pl.BlockSpec(memory_space=pl.ANY)] * len(before)
    first = 3 + len(x_pieces)
    return pl.pallas_call(
        functools.partial(ffn_kernel, len(x_pieces)),
        grid=(pl.cdiv(hidden, tile),),
        in_specs=[block, weight, weight]
        + [pl.BlockSpec(x.shape, lambda n: (0, 0)) for x in x_pieces]
        + kept,
        out_specs=[pl.BlockSpec((count, width), lambda n: (chunk, 0))] + [block] * 3,
        out_shape=[jax.ShapeDtypeStruct((CHUNKS * count, width), BF16)] + [out] * 3,
        input_output_aliases={first + i: i for i in range(len(before))},
        compiler_params=params(),
        cost_estimate=cost(12),
        name="ffn",
    )(act_grad, gate_t, up_t, *x_pieces, *before)


def scatter_kernel(part, place_ref, x_ref, w_ref, out_ref):
    v = dot_nn(x_ref[...], w_ref[...]).astype(BF16)
    for j in range(x_ref.shape[0] // part):
        at = pl.multiple_of(place_ref[j] * part, part)
        out_ref[pl.ds(at, part), :] = v[j * part : (j + 1) * part]


def scattered_product(x, w, part, places):
    count, depth = x.shape
    width = w.shape[1]
    tile = 512
    return pl.pallas_call(
        functools.partial(scatter_kernel, part),
        grid_spec=pltpu.PrefetchScalarGridSpec(
            num_scalar_prefetch=1,
            grid=(width // tile,),
            in_specs=[
                pl.BlockSpec((count, depth), lambda n, place: (0, 0)),
                pl.BlockSpec((depth, tile), lambda n, place: (0, n)),
            ],
            out_specs=pl.BlockSpec((count, tile), lambda n, place: (0, n)),
        ),
        out_shape=jax.ShapeDtypeStruct((count, width), BF16),
        compiler_params=params(),
        cost_estimate=cost(10),
        name="ffn_part",
    )(places, x, w)


def input_back_kernel(terms, flip, part, peers, place_ref, *refs):
    g_refs, w_refs, out_refs = refs[:terms], refs[terms : 2 * terms], refs[2 * terms : -1]
    all_ref = refs[-1]
    product = dot_tt if flip else dot_nn
    total = product(g_refs[0][...], w_refs[0][...])
    for g_ref, w_ref in zip(g_refs[1:], w_refs[1:]):
        total = total + product(g_ref[...], w_ref[...])
    rows = []
    if not flip:
        for m in range(peers):
            for i in range(CHUNKS):
                at = (i * peers + m) * part
                rows.append(total[at : at + part].astype(BF16))
    else:
        all_ref[...] = total
        for m in range(peers):
            for i in range(CHUNKS):
                at = pl.multiple_of(place_ref[i * peers + m] * part, part)
                rows.append(all_ref[pl.ds(at, part), :].astype(BF16))
    for m in range(peers):
        own = rows[m * CHUNKS : (m + 1) * CHUNKS]
        if peers == 4 and m == 3:
            out_refs[3][...] = own[0]
            out_refs[4][...] = own[1]
        else:
            for i in range(CHUNKS):
                out_refs[m][i * part : (i + 1) * part] = own[i]


def input_back(grads, weights, flip, part, peers, places):
    count, depth = grads[0].shape
    width = weights[0].shape[0 if flip else 1]
    tile = 512
    terms = len(grads)
    sizes = [CHUNKS * part] * peers
    if peers == 4:
        sizes = [CHUNKS * part] * 3 + [part] * 2
    weight = (
        pl.BlockSpec((tile, depth), lambda n, place: (n, 0))
        if flip
        else pl.BlockSpec((depth, tile), lambda n, place: (0, n))
    )
    return pl.pallas_call(
        functools.partial(input_back_kernel, terms, flip, part, peers),
        grid_spec=pltpu.PrefetchScalarGridSpec(
            num_scalar_prefetch=1,
            grid=(width // tile,),
            in_specs=[pl.BlockSpec((count, depth), lambda n, place: (0, 0))] * terms
            + [weight] * terms,
            out_specs=[pl.BlockSpec((n_rows, tile), lambda n, place: (0, n)) for n_rows in sizes],
            scratch_shapes=[pltpu.VMEM((count, tile), F32)],
        ),
        out_shape=[jax.ShapeDtypeStruct((n_rows, width), BF16) for n_rows in sizes],
        compiler_params=params(),
        cost_estimate=cost(16),
        name="input_back",
    )(places, *grads, *weights)


def norm_back(term_refs, v, gain, base):
    c = term_refs[0][...].astype(F32)
    for term_ref in term_refs[1:]:
        c = c + term_ref[...].astype(F32)
    inverse = lax.rsqrt(jnp.mean(v * v, axis=-1, keepdims=True) + EPS)
    plain = v * inverse
    scaled = c * gain
    mean = jnp.mean(scaled * plain, axis=-1, keepdims=True)
    return base + inverse * (scaled - plain * mean), jnp.sum(c * plain, axis=0, keepdims=True)


def resid_back_kernel(terms, peers, gain_ref, *refs):
    term_refs = refs[:terms]
    res_refs = refs[terms : terms + CHUNKS]
    up_refs = refs[terms + CHUNKS : terms + 2 * CHUNKS]
    w_refs = refs[terms + 2 * CHUNKS : terms + 2 * CHUNKS + peers]
    grad_ref, low_ref, gain_out = refs[terms + 2 * CHUNKS + peers :][:3]
    g_refs = refs[terms + 2 * CHUNKS + peers + 3 :]
    n = pl.program_id(0)

    @pl.when(n == 0)
    def _():
        v = jnp.concatenate([ref[...] for ref in res_refs], axis=0)
        base = jnp.concatenate([ref[...] for ref in up_refs], axis=0).astype(F32)
        grad, gain_grad = norm_back(term_refs, v, gain_ref[...], base)
        grad_ref[...] = grad
        low_ref[...] = grad.astype(BF16)
        gain_out[...] = gain_grad

    low = low_ref[...]
    for m in range(peers):

        @pl.when(n == m)
        def _(m=m):
            g_refs[m][...] = dot_tt(low, w_refs[m][...]).astype(BF16)


def resid_back(terms, gain, residuals, upstream, weights):
    own, width = terms[0].shape
    part = own // CHUNKS
    peers = len(weights)
    depth = weights[0].shape[0]
    same = lambda shape: pl.BlockSpec(shape, lambda n: (0, 0))
    chunk_of = lambda i: pl.BlockSpec((part, width), lambda n: (i * peers, 0))
    return pl.pallas_call(
        functools.partial(resid_back_kernel, len(terms), peers),
        grid=(peers,),
        in_specs=[same((1, width))]
        + [same((own, width))] * len(terms)
        + [same((part, width))] * CHUNKS
        + [chunk_of(i) for i in range(CHUNKS)]
        + [same((depth, width))] * peers,
        out_specs=[same((own, width)), same((own, width)), same((1, width))]
        + [same((own, depth))] * peers,
        out_shape=[
            jax.ShapeDtypeStruct((own, width), F32),
            jax.ShapeDtypeStruct((own, width), BF16),
            jax.ShapeDtypeStruct((1, width), F32),
        ]
        + [jax.ShapeDtypeStruct((own, depth), BF16)] * peers,
        compiler_params=params(),
        cost_estimate=cost(11),
        name="resid_back",
    )(gain.reshape(1, width), *terms, *residuals, *[upstream] * CHUNKS, *weights)


def token_back_kernel(terms, t_ref, gain_ref, *refs):
    term_refs = refs[:terms]
    tok_refs = refs[terms : terms + CHUNKS]
    base_ref, out_ref, gain_out = refs[terms + CHUNKS :]
    v = jnp.concatenate([ref[...] for ref in tok_refs], axis=0).astype(F32)
    grad, gain_grad = norm_back(term_refs, v, gain_ref[...], base_ref[...])
    out_ref[...] = grad.astype(BF16)
    gain_out[...] = gain_grad


def token_back(terms, gain, tok, resid_grad, t, peers):
    own, width = terms[0].shape
    part = own // CHUNKS
    same = lambda shape: pl.BlockSpec(shape, lambda n, t: (0, 0))
    chunk_of = lambda i: pl.BlockSpec((part, width), lambda n, t: (i * peers + t[0], 0))
    return pl.pallas_call(
        functools.partial(token_back_kernel, len(terms)),
        grid_spec=pltpu.PrefetchScalarGridSpec(
            num_scalar_prefetch=1,
            grid=(1,),
            in_specs=[same((1, width))]
            + [same((own, width))] * len(terms)
            + [chunk_of(i) for i in range(CHUNKS)]
            + [same((own, width))],
            out_specs=[same((own, width)), same((1, width))],
        ),
        out_shape=[
            jax.ShapeDtypeStruct((own, width), BF16),
            jax.ShapeDtypeStruct((1, width), F32),
        ],
        compiler_params=params(),
        cost_estimate=cost(5),
        name="token_back",
    )(t, gain.reshape(1, width), *terms, *[tok] * CHUNKS, resid_grad)


def outer(left, right, k, axis, parts, add=None):
    if axis == 0:
        left = half_columns(left, k)
    else:
        right = half_columns(right, k)
    v = lax.dot_general(left, right, (((0,), (0,)), ((), ())), preferred_element_type=F32)
    if add is not None:
        v = v + add.astype(F32)
    v = v.astype(BF16)
    width = v.shape[1] // parts
    return [v[:, j * width : (j + 1) * width] for j in range(parts)]


def fold_kernel(a_ref, b_ref, out_ref):
    out_ref[...] = (a_ref[...].astype(F32) + b_ref[...].astype(F32)).astype(BF16)


def row_tile(rows):
    return 256 if rows % 256 == 0 else (352 if rows > 352 else rows)


def fold(a, b):
    rows, width = a.shape
    tile = row_tile(rows)
    block = pl.BlockSpec((tile, width), lambda i: (i, 0))
    return pl.pallas_call(
        fold_kernel,
        grid=(pl.cdiv(rows, tile),),
        in_specs=[block, block],
        out_specs=block,
        out_shape=jax.ShapeDtypeStruct(a.shape, BF16),
        input_output_aliases={0: 0},
        compiler_params=params(),
        cost_estimate=cost(1 + rows * width / 4e5),
        name="fold",
    )(a, b)


def pick_kernel(which_ref, a_ref, b_ref, out_ref):
    @pl.when(which_ref[0] == 0)
    def _():
        out_ref[...] = a_ref[...]

    @pl.when(which_ref[0] != 0)
    def _():
        out_ref[...] = b_ref[...]


def pick(which, a, b):
    rows, width = a.shape
    tile = row_tile(rows)
    return pl.pallas_call(
        pick_kernel,
        grid_spec=pltpu.PrefetchScalarGridSpec(
            num_scalar_prefetch=1,
            grid=(pl.cdiv(rows, tile),),
            in_specs=[
                pl.BlockSpec((tile, width), lambda i, which: (i * (1 - which[0]), 0)),
                pl.BlockSpec((tile, width), lambda i, which: (i * which[0], 0)),
            ],
            out_specs=pl.BlockSpec((tile, width), lambda i, which: (i, 0)),
        ),
        out_shape=jax.ShapeDtypeStruct(a.shape, a.dtype),
        compiler_params=params(),
        cost_estimate=cost(1 + rows * width / 5e5),
        name="pick",
    )(jnp.full((1,), which, jnp.int32), a, b)


def reduce_second_kernel(one_ref, two_ref, a_ref, b_ref, x_ref, y_ref):
    n = a_ref.shape[0]
    x_ref[:n] = one_ref[:n]
    x_ref[n:] = (one_ref[n:].astype(F32) + b_ref[...].astype(F32)).astype(BF16)
    y_ref[:n] = (two_ref[:n].astype(F32) + a_ref[...].astype(F32)).astype(BF16)
    y_ref[n:] = two_ref[n:]


def reduce_second(one, two, a, b):
    n, width = one.shape
    tile = 512
    whole = pl.BlockSpec((n, tile), lambda i: (0, i))
    half = pl.BlockSpec((n // 2, tile), lambda i: (0, i))
    return pl.pallas_call(
        reduce_second_kernel,
        grid=(width // tile,),
        in_specs=[whole, whole, half, half],
        out_specs=[whole, whole],
        out_shape=[jax.ShapeDtypeStruct(one.shape, BF16)] * 2,
        compiler_params=params(),
        cost_estimate=cost(2),
        name="reduce_second",
    )(one, two, a, b)


def reorder_kernel(x_ref, out_ref):
    out_ref[...] = x_ref[...]


def true_order(x, peers):
    count, width = x.shape
    part = count // (peers * CHUNKS)
    return pl.pallas_call(
        reorder_kernel,
        grid=(CHUNKS * peers,),
        in_specs=[
            pl.BlockSpec((part, width), lambda i: (i % peers * CHUNKS + i // peers, 0))
        ],
        out_specs=pl.BlockSpec((part, width), lambda i: (i, 0)),
        out_shape=jax.ShapeDtypeStruct(x.shape, x.dtype),
        compiler_params=params(),
        cost_estimate=cost(3),
        name="true_order",
    )(x)


def unite_kernel(parts, axis, k_ref, *refs):
    mine, theirs, out_ref = refs[:parts], refs[parts : 2 * parts], refs[-1]
    first = k_ref[0] == 0
    if axis == 0:
        first = first == (pl.program_id(0) < pl.num_programs(0) // 2)
        out_ref[...] = jnp.where(first, mine[0][...], theirs[0][...]).astype(F32)
        return
    width = mine[0].shape[1]
    for j in range(parts):
        a, b = mine[j][...].astype(F32), theirs[j][...].astype(F32)
        out_ref[:, j * width : (j + 1) * width] = jnp.where(first, a, b)
        at = (parts + j) * width
        out_ref[:, at : at + width] = jnp.where(first, b, a)


def unite(mine, theirs, k, axis):
    parts = len(mine)
    rows, width = mine[0].shape
    tile = 128 if rows % 128 else 256
    steps = pl.cdiv(rows, tile)
    if axis == 0:
        grid, shape = (2 * steps,), (2 * rows, width)
        half_at = lambda i, k: (i % steps, 0)
    else:
        grid, shape = (steps,), (rows, 2 * parts * width)
        half_at = lambda i, k: (i, 0)
    return pl.pallas_call(
        functools.partial(unite_kernel, parts, axis),
        grid_spec=pltpu.PrefetchScalarGridSpec(
            num_scalar_prefetch=1,
            grid=grid,
            in_specs=[pl.BlockSpec((tile, width), half_at)] * (2 * parts),
            out_specs=pl.BlockSpec((tile, shape[1]), lambda i, k: (i, 0)),
        ),
        out_shape=jax.ShapeDtypeStruct(shape, F32),
        compiler_params=params(),
        cost_estimate=cost(1.5 + shape[0] * shape[1] / 7e5),
        name="unite",
    )(jnp.full((1,), k, jnp.int32), *mine, *theirs)


def half_columns(x, k):
    width = x.shape[1] // 2
    return lax.dynamic_slice_in_dim(x, k * width, width, 1)


def per_device(
    tokens,
    positions,
    w_query,
    w_key,
    w_value,
    w_out,
    w_gate,
    w_up,
    w_down,
    gain_attn,
    gain_ffn,
    cotangent,
):
    rows, span, width = tokens.shape
    count = rows * span
    peers = lax.axis_size("tp")
    t = lax.axis_index("tp")
    reach = WINDOW // span
    flat = w_query.shape[1]
    heads = flat // HEAD
    hidden = w_gate.shape[1]
    chunk = count // CHUNKS
    chunk_rows = rows // CHUNKS
    part = chunk // peers
    order = Order()

    def piece(x, i, m):
        return lax.dynamic_slice_in_dim(x, i * chunk + (t ^ m) * part, part, 0)

    tok = tokens.reshape(count, width)
    cot = cotangent.reshape(count, width)

    t_arg = jnp.full((1,), t, jnp.int32)
    gate_t, up_t = w_gate.T, w_up.T
    out_rows = [w_out] + [tp_send(w_out, m) for m in range(1, min(peers, 3))]

    within = jnp.arange(span, dtype=jnp.int32)[None, :]
    low = jnp.maximum(within - positions, within - (WINDOW - 1))
    low_col = low.reshape(count, 1)
    low_rows = low.astype(F32).reshape(rows, 1, span)
    half_size = HEAD // 2
    freq = THETA ** (-jnp.arange(half_size, dtype=F32) / half_size)
    freq = jnp.concatenate([freq, freq])
    sign = jnp.concatenate([-jnp.ones(half_size, F32), jnp.ones(half_size, F32)])
    angles = positions.reshape(count, 1).astype(F32) * freq
    tables = (jnp.cos(angles), jnp.sin(angles) * sign)

    weights_kv = (w_key, w_value)
    normed_attn, pair_0 = project(
        tok, tables, gain_attn, weights_kv, (True, False), 0, chunk, True
    )
    order.mark(pair_0)
    far_0 = seq_shift(pair_0, 2)
    normed_attn, pair_1 = project(
        order.gate(tok), tables, gain_attn, weights_kv, (True, False), chunk, chunk, True,
        normed_attn,
    )
    order.mark(pair_1)
    pairs = [pair_0, pair_1]
    (queries,) = project(order.gate(normed_attn), tables, gain_attn, (w_query,), (True,), 0, count)
    order.mark(queries)
    q_far = seq_shift(queries, -2)

    def two_more(spans, far, sign):
        between = between_spans(spans[-1], far, sign)
        spans += [between, far]
        return seq_shift(far, 2 * sign) if len(spans) < reach + 1 else None

    spans = [[pair_0], [pair_1]]
    far_0 = order.gate(far_0)
    order.mark(far_0)
    next_0 = two_more(spans[0], far_0, 1)
    upstream_low, act_grad = act_grad_of(order.gate(cot), w_down, t_arg, peers)
    order.mark(act_grad)
    q_far = order.gate(q_far)
    order.mark(q_far)
    q_spans = [queries]
    q_next = two_more(q_spans, q_far, -1)

    if peers == 4:
        half = w_out.shape[0] // 2
        out_1, out_2 = order.gate(*out_rows[1:])
        order.mark(out_1, out_2)
        out_3 = (tp_send(out_1[:half], 2), tp_send(out_2[half:], 1))
    else:
        out_rows += [tp_send(w_out, m) for m in range(3, peers)]

    while next_0 is not None:
        far_0 = order.gate(next_0)
        order.mark(far_0)
        next_0 = two_more(spans[0], far_0, 1)
    far_1 = seq_shift(order.gate(pair_1), 2)

    def attention(i, before):
        gated = order.gate(*spans[i])
        mixed, lse = attend(queries, gated, low_col, chunk_rows, i * chunk_rows, before)
        order.mark(mixed)
        sent = split_near(mixed, t_arg, peers, i)
        order.mark(*sent)
        return mixed, lse, [sent[0]] + [tp_send(sent[m], m) for m in range(1, peers)]

    mixed_0, lse_0, pieces_0 = attention(0, ())

    far_1 = order.gate(far_1)
    order.mark(far_1)
    next_1 = two_more(spans[1], far_1, 1)

    if peers == 4:
        out_3 = jnp.concatenate(order.gate(*out_3), axis=0)
        order.mark(out_3)
        out_rows.append(out_3)

    def residual_step(i, pieces):
        pieces = order.gate(*pieces)
        residual, normed = residual_of(piece(tok, i, 0), gain_ffn, pieces, out_rows)
        order.mark(residual)
        return residual, tp_gather(normed)

    residual_0, gathered_0 = residual_step(0, pieces_0)

    while q_next is not None:
        q_far = order.gate(q_next)
        order.mark(q_far)
        q_next = two_more(q_spans, q_far, -1)
    while next_1 is not None:
        far_1 = order.gate(next_1)
        order.mark(far_1)
        next_1 = two_more(spans[1], far_1, 1)
    mixed, lse_1, pieces_1 = attention(1, (mixed_0,))

    def ffn_step(i, gathered, before):
        outs = ffn(order.gate(*gathered), act_grad, gate_t, up_t, i, before)
        order.mark(outs[0])
        return outs

    ffn_0 = ffn_step(0, gathered_0, ())
    residual_1, gathered_1 = residual_step(1, pieces_1)
    normed_ffn, activated, gate_grad, up_grad = ffn_step(1, gathered_1, tuple(ffn_0))

    sum_down = LineSum(order, activated, upstream_low, 1, 2)
    sum_gate = LineSum(order, gate_grad, normed_ffn, 1, 2)
    sum_up = LineSum(order, up_grad, normed_ffn, 1, 2)
    sum_down.begin()
    sum_gate.begin()
    sum_down.own()
    sum_down.launch(0)
    sum_down.launch(1)
    near = jnp.arange(CHUNKS * peers, dtype=jnp.int32)
    true = (jnp.arange(CHUNKS)[:, None] * peers + (t ^ jnp.arange(peers))).reshape(-1)
    true = true.astype(jnp.int32)
    gate_g, up_g = order.gate(gate_grad, up_grad)
    ffn_back = input_back([gate_g, up_g], [gate_t, up_t], False, part, peers, near)
    order.mark(*ffn_back)
    reduce_ffn = TpReduce(ffn_back)
    sum_gate.own()
    sum_down.step(0)
    sum_gate.launch(0)
    reduce_ffn.second(order)
    sum_up.begin()
    places = ((t ^ jnp.arange(peers)) * CHUNKS + jnp.arange(CHUNKS)[:, None]).reshape(-1)
    ffn_part = scattered_product(order.gate(activated), w_down, part, places.astype(jnp.int32))
    order.mark(ffn_part)
    sum_down.step(1)
    sum_gate.launch(1)

    terms = order.gate(*reduce_ffn.terms())
    resid_grad, resid_low, gain_ffn_grad, *grads_own = resid_back(
        terms, gain_ffn, [residual_0, residual_1], upstream_low, out_rows
    )
    order.mark(resid_low)
    grads_got = [grads_own[0]] + [tp_send(grads_own[m], m) for m in range(1, peers)]
    resid_all = lax.all_gather(resid_low, "tp", axis=0, tiled=True)
    sum_down.step(0)
    sum_up.own()

    mixed_grad = join_true(
        order.gate(*grads_got), mixed, [lse_0, lse_1], low_rows, t_arg
    )
    order.mark(mixed_grad)
    g_far = seq_shift(mixed_grad, -2)
    sum_gate.step(0)
    sum_up.launch(0)
    ffn_part = lax.optimization_barrier((ffn_part, resid_all))[0]
    out_sum = lax.psum_scatter(ffn_part, "tp", scatter_dimension=0, tiled=True)

    def query_step(i, lse_i, before):
        grad_g = order.gate(mixed_grad)
        query_grad = query_back(
            queries, grad_g, mixed, spans[i], lse_i, low_col, tables, chunk_rows,
            i * chunk_rows, before,
        )
        order.mark(query_grad)
        return query_grad

    query_grad = query_step(0, lse_0, ())
    sum_down.step(1)
    sum_gate.step(1)
    sum_up.launch(1)
    query_grad = query_step(1, lse_1, (query_grad,))
    sum_down.step(0)
    sum_query = LineSum(order, normed_attn, query_grad, 0)
    sum_query.begin()
    sum_gate.step(0)

    g_far = order.gate(g_far)
    order.mark(g_far)
    g_spans = [mixed_grad]
    g_next = two_more(g_spans, g_far, -1)
    sum_down.step(1)
    sum_query.own()
    sum_up.step(0)
    sum_query.launch()
    sum_gate.step(1)
    mixed_by_t = jnp.transpose(mixed.reshape(CHUNKS, peers, part, flat), (1, 0, 2, 3))
    sum_out = LineSum(order, mixed_by_t.reshape(count, flat), resid_all, 0)
    while g_next is not None:
        g_far = order.gate(g_next)
        order.mark(g_far)
        g_next = two_more(g_spans, g_far, -1)
    sum_out.begin()
    sum_up.step(1)
    sum_gate.step(0)
    sum_out.own()
    sum_out.launch()

    g_spans = list(order.gate(*g_spans))
    order.mark(*g_spans)
    key_value = ()
    for i in range(CHUNKS):
        g_first = order.gate(g_spans[0])
        key_value = key_back(
            pairs[i], q_spans, [g_first] + g_spans[1:], tables, chunk_rows, i * chunk_rows,
            tuple(key_value),
        )
        order.mark(*key_value)
        if i == 0:
            sum_up.step(0)
            sum_query.step()
    key_grad, value_grad = key_value
    sum_key = LineSum(order, normed_attn, key_grad, 0)
    sum_value = LineSum(order, normed_attn, value_grad, 0)
    sum_key.begin()
    sum_value.begin()
    sum_key.own()
    sum_key.launch()
    sum_gate.step(1)

    key_g, value_g, query_g = order.gate(key_grad, value_grad, query_grad)
    attn_back = input_back(
        [query_g, key_g, value_g], [w_query, w_key, w_value], True, part, peers, true
    )
    order.mark(*attn_back)
    reduce_attn = TpReduce(attn_back)
    sum_value.own()
    sum_value.launch()
    sum_up.step(1)
    sum_out.step()
    reduce_attn.second(order)
    full_down = sum_down.finish()
    sum_up.step(0)
    sum_query.step()
    sum_key.step()
    full_gate = sum_gate.finish()

    terms = order.gate(*reduce_attn.terms())
    token_grad, gain_attn_grad = token_back(terms, gain_attn, tok, resid_grad, t_arg, peers)
    order.mark(token_grad)
    residual = jnp.concatenate([residual_0, residual_1], axis=0)
    output = (residual + out_sum.astype(F32)).astype(BF16)

    def gathered(own):
        whole = lax.all_gather(own, "tp", axis=0, tiled=True)
        return true_order(whole, peers).reshape(rows, span, width)

    token_grad = gathered(token_grad)
    output = gathered(output)
    gain_grads = total_over_all(jnp.concatenate([gain_attn_grad, gain_ffn_grad], axis=0))

    sum_value.step()
    sum_up.step(1)
    sum_out.step()
    sum_query.step()
    sum_key.step()
    full_up = sum_up.finish()
    sum_value.step()
    sum_out.step()
    full_query = sum_query.finish()
    sum_key.step()
    full_out = sum_out.finish()
    sum_value.step()
    full_key = sum_key.finish()
    full_value = sum_value.finish()
    return (
        output,
        token_grad,
        full_query,
        full_key,
        full_value,
        full_out,
        full_gate.T,
        full_up.T,
        full_down,
        gain_grads[0],
        gain_grads[1],
    )


def solution(mesh):
    return jax.shard_map(
        per_device,
        mesh=mesh,
        in_specs=(
            P(None, "seq", None),
            P(None, "seq"),
            P(None, "tp"),
            P(None, "tp"),
            P(None, "tp"),
            P("tp", None),
            P(None, "tp"),
            P(None, "tp"),
            P("tp", None),
            P(),
            P(),
            P(None, "seq", None),
        ),
        out_specs=(
            P(None, "seq", None),
            P(None, "seq", None),
            P(None, "tp"),
            P(None, "tp"),
            P(None, "tp"),
            P("tp", None),
            P(None, "tp"),
            P(None, "tp"),
            P("tp", None),
            P(),
            P(),
        ),
        check_vma=False,
    )
```
